128 devices in a mesh: img: 32 (over z_lo, y, x), layer: 4 (over z_hi, core).
Axes of the slice: x: 4, y: 4, z: 4 (z_hi: 2, z_lo: 2; z = z_hi * 2 + z_lo), core: 2. Of those that a mesh axis runs over, the one named last changes fastest.
Arguments:
- checkpoint: bfloat16 [4, 16384, 2048], P('layer', 'img'), may hold values from -6 to 6
- cotangent: bfloat16 [4, 16384, 2048], P('layer', 'img')
- weights: bfloat16 [8, 2048, 2048], P('layer'), may hold values from -0.1875 to 0.1875
- partner: int32 [32], P('img'), may hold values from 0 to 31, as said below
Outputs:
- self_tile: float32 [16384, 512], P(('img', 'layer'))
- cross_tile: float32 [16384, 512], P(('img', 'layer'))
The draws below stay inside these ranges and needn't reach their ends.
Inputs may be any that keep to these rules, and one draw needn't show every extreme that they name: partner[p] = p XOR r for one round number r with 1 <= r < 32, the same r for every p.
All inputs are finite; a program needn't handle non-finite values.
Results may differ from the reference program's by a relative error of at most 0.00051.
Values may be sent and summed in bfloat16 or wider, within the bound.
A program may use at most 128 MiB of HBM per device.

```python
import jax
import jax.numpy as jnp
from jax import lax

D = 2048
LG = 2
IMG_DEV = 512
IMAGES = 16384
LAYERS = 8
N_IMG = 32
N_LAYER = 4


def draw_partner(key, part):
    key = jax.random.fold_in(key, 5)
    round_number = jax.random.randint(key, (), 1, N_IMG, dtype=jnp.int32)
    return jnp.bitwise_xor(jnp.arange(N_IMG, dtype=jnp.int32), round_number)


def draw_cotangent(key, part):
    key_common = jax.random.fold_in(key, 11)
    key_noise = jax.random.fold_in(key, 12)
    common = jax.random.normal(key_common, (N_LAYER, 1, D), jnp.float32)
    noise = jax.random.normal(key_noise, (N_LAYER, IMAGES, D), jnp.float32)
    return (0.8 * common + 0.6 * noise).astype(jnp.bfloat16)


def levels(stream_key, shape, pieces, smallest, high):
    factor_of, own = 1.0, jax.random.fold_in(stream_key, 6)
    for position, shards_of in pieces:
        heights = jnp.exp(jax.random.uniform(jax.random.fold_in(own, position), (shards_of,), jnp.float32, smallest / len(pieces), high / len(pieces)))
        factor_of = factor_of * jnp.repeat(heights, shape[position] // shards_of).reshape([-1 if axis == position else 1 for axis in range(len(shape))])
    return factor_of


def centred(key, shape, width, limit, shards=(), kind=jnp.bfloat16):
    drawn = jax.random.normal(key, shape, jnp.float32) * width
    if len(shards) > 0:
        drawn = levels(key, shape, shards, -0.22, 0.18) * drawn
    return jnp.clip(drawn, min=-limit, max=limit).astype(kind)


def setup_inputs(seed: int = 0) -> dict:
    key_list = jax.random.split(jax.random.key(seed), 5)
    return {
        "checkpoint": centred(key_list[0], (N_LAYER, IMAGES, D), 1.0, 6.0, ((0, 4), (1, 32))),
        "cotangent": draw_cotangent(jax.random.fold_in(key_list[4], 71), 0),
        "weights": centred(key_list[2], (LAYERS, D, D), (D // 2) ** -0.5, 0.1875, ((0, 4),)),
        "partner": draw_partner(jax.random.fold_in(key_list[4], 71), 0),
    }


def derivative(z):
    s = jax.nn.sigmoid(z)
    return s * (1.0 + z * (1.0 - s))


def group_pass(start, cotan, layer_weights):
    acts = [start]
    zlist = []
    a = start
    for k in range(LG):
        z = jnp.dot(a, layer_weights[k], preferred_element_type=jnp.float32)
        zlist.append(z)
        if k < LG - 1:
            a = (z * jax.nn.sigmoid(z)).astype(jnp.bfloat16)
            acts.append(a)
    grads = [None] * LG
    upper = cotan.astype(jnp.float32)
    for k in range(LG - 1, -1, -1):
        g = (upper * derivative(zlist[k])).astype(jnp.bfloat16)
        grads[k] = g
        if k > 0:
            upper = lax.dot_general(g, layer_weights[k], (((1,), (1,)), ((), ())), preferred_element_type=jnp.float32)
    return jnp.stack(acts), jnp.stack(grads)


def reference(checkpoint, cotangent, weights, partner):
    self_sum = jnp.zeros((N_IMG, IMG_DEV, IMG_DEV), jnp.float32)
    cross_sum = jnp.zeros((N_IMG, IMG_DEV, IMG_DEV), jnp.float32)
    for q in range(N_LAYER):
        acts, grads = group_pass(checkpoint[q], cotangent[q], weights[q * LG:(q + 1) * LG])
        acts = acts.reshape(LG, N_IMG, IMG_DEV, D).astype(jnp.float32)
        grads = grads.reshape(LG, N_IMG, IMG_DEV, D).astype(jnp.float32)
        acts_p = jnp.take(acts, partner, axis=1)
        grads_p = jnp.take(grads, partner, axis=1)
        for k in range(LG):
            ga = jnp.einsum('nbd,ncd->nbc', acts[k], acts[k]) / D
            gg = jnp.einsum('nbd,ncd->nbc', grads[k], grads[k]) / D
            self_sum = self_sum + ga * gg
            ca = jnp.einsum('nbd,ncd->nbc', acts[k], acts_p[k]) / D
            cg = jnp.einsum('nbd,ncd->nbc', grads[k], grads_p[k]) / D
            cross_sum = cross_sum + ca * cg
    return self_sum.reshape(IMAGES, IMG_DEV), cross_sum.reshape(IMAGES, IMG_DEV)
```

```python
import functools

import jax
import jax.numpy as jnp
from jax import lax
from jax.experimental import pallas as pl
from jax.experimental.pallas import tpu as pltpu
from jax.sharding import PartitionSpec as P

MESH = pl.DeviceIdType.MESH


def paired(index, round_number):
    out = index
    bit = 0
    while round_number >> bit:
        if (round_number >> bit) & 1:
            out = out + (1 - 2 * ((index // (1 << bit)) % 2)) * (1 << bit)
        bit += 1
    return out


def swap_kernel(round_number, a_ref, c_ref, a_out, c_out, send, recv):
    other = paired(lax.axis_index("img"), round_number)
    device = (other, lax.axis_index("layer"))
    barrier = pltpu.get_barrier_semaphore()
    pl.semaphore_signal(barrier, inc=1, device_id=device, device_id_type=MESH)
    pl.semaphore_wait(barrier, 1)
    copies = [
        pltpu.make_async_remote_copy(
            src_ref=src, dst_ref=dst, send_sem=send.at[n], recv_sem=recv.at[n],
            device_id=device, device_id_type=MESH,
        )
        for n, (src, dst) in enumerate(((a_ref, a_out), (c_ref, c_out)))
    ]
    for copy in copies:
        copy.start()
    for copy in copies:
        copy.wait()


def swap(round_number, a, c):
    return pl.pallas_call(
        functools.partial(swap_kernel, round_number),
        out_shape=[jax.ShapeDtypeStruct(a.shape, a.dtype)] * 2,
        in_specs=[pl.BlockSpec(memory_space=pl.ANY)] * 2,
        out_specs=[pl.BlockSpec(memory_space=pl.ANY)] * 2,
        scratch_shapes=[pltpu.SemaphoreType.DMA((2,)), pltpu.SemaphoreType.DMA((2,))],
        compiler_params=pltpu.CompilerParams(collective_id=round_number, has_side_effects=True),
        name=f"swap_{round_number}",
    )(a, c)


def derivative(z):
    s = jax.nn.sigmoid(z)
    return s * (1.0 + z * (1.0 - s))


def group_pass(start, cotan, layer_weights):
    depth = layer_weights.shape[0]
    acts = [start]
    zlist = []
    a = start
    for k in range(depth):
        z = jnp.dot(a, layer_weights[k], preferred_element_type=jnp.float32)
        zlist.append(z)
        if k < depth - 1:
            a = (z * jax.nn.sigmoid(z)).astype(jnp.bfloat16)
            acts.append(a)
    grads = [None] * depth
    upper = cotan.astype(jnp.float32)
    for k in range(depth - 1, -1, -1):
        g = (upper * derivative(zlist[k])).astype(jnp.bfloat16)
        grads[k] = g
        if k > 0:
            upper = lax.dot_general(
                g, layer_weights[k], (((1,), (1,)), ((), ())), preferred_element_type=jnp.float32
            )
    return acts, grads


def kernel_tile(acts, grads, other_acts, other_grads):
    width = acts[0].shape[1]
    nt = (((1,), (1,)), ((), ()))
    total = 0.0
    for a, g, b, h in zip(acts, grads, other_acts, other_grads):
        gram_a = lax.dot_general(a, b, nt, preferred_element_type=jnp.float32) / width
        gram_g = lax.dot_general(g, h, nt, preferred_element_type=jnp.float32) / width
        total = total + gram_a * gram_g
    return total


def on_device(checkpoint, cotangent, weights, partner):
    start, cotan = checkpoint[0], cotangent[0]
    round_number = jnp.bitwise_xor(partner[0], lax.axis_index("img"))
    n = lax.axis_size("img")
    other_start, other_cotan = lax.switch(
        round_number - 1, [functools.partial(swap, r) for r in range(1, n)], start, cotan
    )
    acts, grads = group_pass(start, cotan, weights)
    self_term = kernel_tile(acts, grads, acts, grads)
    other_acts, other_grads = group_pass(other_start, other_cotan, weights)
    cross_term = kernel_tile(acts, grads, other_acts, other_grads)
    self_tile = lax.psum_scatter(self_term, "layer", scatter_dimension=0, tiled=True)
    cross_tile = lax.psum_scatter(cross_term, "layer", scatter_dimension=0, tiled=True)
    return (self_tile, cross_tile)


def solution(mesh):
    return jax.shard_map(
        on_device,
        mesh=mesh,
        in_specs=(
            P("layer", "img", None),
            P("layer", "img", None),
            P("layer", None, None),
            P("img"),
        ),
        out_specs=(P(("img", "layer"), None), P(("img", "layer"), None)),
        check_vma=False,
    )
```

```python
import functools

import jax
import jax.numpy as jnp
from jax import lax
from jax.experimental import pallas as pl
from jax.experimental.pallas import tpu as pltpu
from jax.sharding import PartitionSpec as P

MESH = pl.DeviceIdType.MESH
F32 = jnp.float32
BF16 = jnp.bfloat16
NN = (((1,), (0,)), ((), ()))
NT = (((1,), (1,)), ((), ()))


def paired(index, round_number):
    out = index
    bit = 0
    while round_number >> bit:
        if (round_number >> bit) & 1:
            out = out + (1 - 2 * ((index // (1 << bit)) % 2)) * (1 << bit)
        bit += 1
    return out


def silu(z):
    return z * jax.nn.sigmoid(z)


def dsilu(z):
    s = jax.nn.sigmoid(z)
    return s * (1.0 + z * (1.0 - s))


def dot(a, b, dims):
    return lax.dot_general(a, b, dims, preferred_element_type=F32)


def round_kernel(
    round_number, n_layer, a_hbm, c_hbm, w_hbm, self_out, cross_out,
    w, x, z, own_sum, gram, block_out, piece_out, self_in, cross_in,
    w_sem, load_sem, in_send, in_recv, self_send, self_recv,
    block_send, block_recv, piece_send, piece_recv,
):
    rows, width = a_hbm.shape
    part = rows // n_layer
    half = rows // 2
    step = width // 4
    scale = 1.0 / width

    img = lax.axis_index("img")
    q = lax.axis_index("layer")
    other = paired(img, round_number)
    low = (round_number & -round_number).bit_length() - 1
    side = (img // (1 << low)) % 2
    holds = (side + q) % 2 == 0

    loads = [
        pltpu.make_async_copy(a_hbm, x.at[0, 0], load_sem.at[0]),
        pltpu.make_async_copy(c_hbm, x.at[0, 3], load_sem.at[1]),
    ]
    w_loads = [
        pltpu.make_async_copy(
            w_hbm.at[k, :, pl.ds(n * step, step)], w.at[k, :, pl.ds(n * step, step)], w_sem.at[k, n]
        )
        for k in range(2)
        for n in range(4)
    ]
    loads[0].start()
    w_loads[0].start()

    barrier = pltpu.get_barrier_semaphore()
    for t in range(1, n_layer):
        pl.semaphore_signal(barrier, inc=1, device_id=(img, (q + t) % n_layer), device_id_type=MESH)
    for t in range(n_layer):
        pl.semaphore_signal(barrier, inc=1, device_id=(other, (q + t) % n_layer), device_id_type=MESH)
    for copy in w_loads[1:4]:
        copy.start()
    loads[1].start()
    for copy in w_loads[4:]:
        copy.start()
    pl.semaphore_wait(barrier, 2 * n_layer - 1)

    def incoming(n):
        source, slot, first = ((a_hbm, 0, 0), (a_hbm, 0, half), (c_hbm, 3, 0), (c_hbm, 3, half))[n]
        return pltpu.make_async_remote_copy(
            src_ref=source.at[pl.ds(first, half)], dst_ref=x.at[1, slot, pl.ds(first, half)],
            send_sem=in_send.at[n], recv_sem=in_recv.at[n],
            device_id=(other, q), device_id_type=MESH,
        )

    @pl.when(jnp.logical_not(holds))
    def _():
        for n in range(4):
            incoming(n).start()

    def forward(p, load):
        for k in range(2):
            def columns(n, carry, k=k):
                at = pl.ds(pl.multiple_of(n * step, step), step)
                if load:
                    pltpu.make_async_copy(w_hbm.at[k, :, at], w.at[k, :, at], w_sem.at[k, n]).wait()
                v = dot(x[p, k], w[k, :, at], NN)
                z[k, :, at] = v
                if k == 0:
                    x[p, 1, :, at] = silu(v).astype(BF16)
                return carry
            lax.fori_loop(0, 4, columns, 0)

    def backward(p, first, count):
        at = pl.ds(first, count)
        x[p, 3, at, :] = (x[p, 3, at, :].astype(F32) * dsilu(z[1, at, :])).astype(BF16)

        def columns(n, carry):
            cols = pl.ds(pl.multiple_of(n * step, step), step)
            u = dot(x[p, 3, at, :], w[1, cols, :], NT)
            x[p, 2, at, cols] = (u * dsilu(z[0, at, cols])).astype(BF16)
            return carry
        lax.fori_loop(0, 4, columns, 0)

    def self_copy(t):
        to = (q + t) % n_layer
        return pltpu.make_async_remote_copy(
            src_ref=own_sum.at[pl.ds(pl.multiple_of(to * part, part), part)], dst_ref=self_in.at[q],
            send_sem=self_send.at[t], recv_sem=self_recv.at[q],
            device_id=(img, to), device_id_type=MESH,
        )

    def self_arrival(source):
        return pltpu.make_async_remote_copy(
            src_ref=own_sum.at[pl.ds(0, part)], dst_ref=self_in.at[source],
            send_sem=self_send.at[0], recv_sem=self_recv.at[source],
            device_id=(img, source), device_id_type=MESH,
        )

    loads[0].wait()
    forward(0, True)
    loads[1].wait()
    backward(0, 0, rows)
    own_sum[...] = (
        (dot(x[0, 0], x[0, 0], NT) * scale) * (dot(x[0, 2], x[0, 2], NT) * scale)
        + (dot(x[0, 1], x[0, 1], NT) * scale) * (dot(x[0, 3], x[0, 3], NT) * scale)
    )
    for t in range(1, n_layer):
        self_copy(t).start()

    def block_copy(b, source):
        return pltpu.make_async_remote_copy(
            src_ref=block_out.at[b], dst_ref=cross_in.at[source],
            send_sem=block_send.at[b], recv_sem=block_recv.at[source],
            device_id=(other, b), device_id_type=MESH,
        )

    def piece_copy(b, t, source):
        to = (q + t) % n_layer
        return pltpu.make_async_remote_copy(
            src_ref=piece_out.at[b, pl.ds(pl.multiple_of(to * part, part), part)],
            dst_ref=cross_in.at[source, :, pl.ds(b * part, part)],
            send_sem=piece_send.at[b, t], recv_sem=piece_recv.at[source, b],
            device_id=(img, to), device_id_type=MESH,
        )

    @pl.when(holds)
    def _():
        incoming(0).wait_recv()
        incoming(1).wait_recv()
        forward(1, False)
        gram[0] = dot(x[0, 0], x[1, 0], NT) * scale
        gram[1] = dot(x[0, 1], x[1, 1], NT) * scale
        for h in range(2):
            incoming(2 + h).wait_recv()
            backward(1, h * half, half)
            at = pl.ds(h * half, half)
            tile = (
                gram[0, :, at] * (dot(x[0, 2], x[1, 2, at, :], NT) * scale)
                + gram[1, :, at] * (dot(x[0, 3], x[1, 3, at, :], NT) * scale)
            )
            for i in range(2):
                b = 2 * h + i
                piece = tile[:, i * part:(i + 1) * part]
                piece_out[b] = piece
                block_out[b] = piece.T
                block_copy(b, q).start()
                for t in range(1, n_layer):
                    piece_copy(b, t, q).start()
                cross_in[q, :, pl.ds(b * part, part)] = piece_out[b, pl.ds(pl.multiple_of(q * part, part), part), :]

    total = own_sum[pl.ds(pl.multiple_of(q * part, part), part), :]
    for t in range(1, n_layer):
        source = (q + t) % n_layer
        self_arrival(source).wait_recv()
        total = total + self_in[source]
    self_out[...] = total

    for source in range(n_layer):
        near = (side + source) % 2 == 0

        @pl.when(jnp.logical_and(near, q != source))
        def _():
            for b in range(n_layer):
                piece_copy(b, 1, source).wait_recv()

        @pl.when(jnp.logical_not(near))
        def _():
            block_copy(0, source).wait_recv()

    cross_out[...] = (cross_in[0] + cross_in[1]) + (cross_in[2] + cross_in[3])

    for t in range(1, n_layer):
        self_copy(t).wait_send()

    @pl.when(holds)
    def _():
        for b in range(n_layer):
            block_copy(b, q).wait_send()
            for t in range(1, n_layer):
                piece_copy(b, t, q).wait_send()

    @pl.when(jnp.logical_not(holds))
    def _():
        for n in range(4):
            incoming(n).wait_send()


def one_round(round_number, n_layer, a, c, w):
    rows, width = a.shape
    part = rows // n_layer
    dma = pltpu.SemaphoreType.DMA
    tile = jax.ShapeDtypeStruct((part, rows), F32)
    return pl.pallas_call(
        functools.partial(round_kernel, round_number, n_layer),
        out_shape=[tile, tile],
        in_specs=[pl.BlockSpec(memory_space=pl.ANY)] * 3,
        out_specs=[pl.BlockSpec(memory_space=pltpu.VMEM)] * 2,
        scratch_shapes=[
            pltpu.VMEM(w.shape, BF16),
            pltpu.VMEM((2, 4, rows, width), BF16),
            pltpu.VMEM((2, rows, width), F32),
            pltpu.VMEM((rows, rows), F32),
            pltpu.VMEM((2, rows, rows), F32),
            pltpu.VMEM((n_layer, part, rows), F32),
            pltpu.VMEM((n_layer, rows, part), F32),
            pltpu.VMEM((n_layer, part, rows), F32),
            pltpu.VMEM((n_layer, part, rows), F32),
            dma((2, 4)), dma((2,)), dma((4,)), dma((4,)), dma((n_layer,)), dma((n_layer,)),
            dma((n_layer,)), dma((n_layer,)), dma((n_layer, n_layer)), dma((n_layer, n_layer)),
        ],
        compiler_params=pltpu.CompilerParams(
            collective_id=round_number, has_side_effects=True, vmem_limit_bytes=60 << 20
        ),
        cost_estimate=pl.CostEstimate(
            flops=8 * rows * width * width + 16 * rows * rows * width,
            bytes_accessed=2 * (w.size + 2 * a.size), transcendentals=4 * a.size,
        ),
        name=f"round_{round_number}",
    )(a, c, w)


def on_device(checkpoint, cotangent, weights, partner):
    round_number = jnp.bitwise_xor(partner[0], lax.axis_index("img"))
    n, n_layer = lax.axis_size("img"), lax.axis_size("layer")
    return tuple(
        lax.switch(
            round_number - 1,
            [functools.partial(one_round, r, n_layer) for r in range(1, n)],
            checkpoint[0], cotangent[0], weights,
        )
    )


def solution(mesh):
    return jax.shard_map(
        on_device,
        mesh=mesh,
        in_specs=(
            P("layer", "img", None),
            P("layer", "img", None),
            P("layer", None, None),
            P("img"),
        ),
        out_specs=(P(("img", "layer"), None), P(("img", "layer"), None)),
        check_vma=False,
    )
```

```python
import functools

import jax
import jax.numpy as jnp
from jax import lax
from jax.experimental import pallas as pl
from jax.experimental.pallas import tpu as pltpu
from jax.sharding import PartitionSpec as P

MESH = pl.DeviceIdType.MESH
F32 = jnp.float32
BF16 = jnp.bfloat16
NN = (((1,), (0,)), ((), ()))
NT = (((1,), (1,)), ((), ()))


def bit_of(index, bit):
    return lax.rem(lax.div(index, 1 << bit), 2)


def paired(index, round_number):
    out = index
    bit = 0
    while round_number >> bit:
        if (round_number >> bit) & 1:
            out = out + (1 - 2 * bit_of(index, bit)) * (1 << bit)
        bit += 1
    return out


def dot(a, b, dims):
    return lax.dot_general(a, b, dims, preferred_element_type=F32)


def round_kernel(
    round_number, n_layer, a_hbm, c_hbm, w_hbm, self_out, cross_out,
    x, d, gram, sums, piece_out, self_in, cross_in,
    w_sem, load_sem, in_send, in_recv, self_send, self_recv,
    block_send, block_recv, piece_send, piece_recv,
):
    rows, width = a_hbm.shape
    part = rows // n_layer
    half = rows // 2
    step = width // 4
    scale = 1.0 / width
    first_w = 8 * rows
    spare = first_w + 2 * width

    img = lax.axis_index("img")
    q = lax.axis_index("layer")
    other = paired(img, round_number)
    low = (round_number & -round_number).bit_length() - 1
    side = bit_of(img, low)
    holds = lax.rem(side + q, 2) == 0

    def w_load(j):
        k, n = lax.div(j, 4), lax.rem(j, 4)
        at = pl.ds(pl.multiple_of(n * step, step), step)
        return pltpu.make_async_copy(
            w_hbm.at[k, :, at],
            x.at[pl.ds(pl.multiple_of(first_w + k * width, width), width), at],
            w_sem.at[j],
        )

    loads = [
        pltpu.make_async_copy(a_hbm, x.at[pl.ds(0, rows)], load_sem.at[0]),
        pltpu.make_async_copy(c_hbm, x.at[pl.ds(3 * rows, rows)], load_sem.at[1]),
    ]
    loads[0].start()
    w_load(0).start()

    barrier = pltpu.get_barrier_semaphore()

    @pl.loop(0, n_layer)
    def _(t):
        to = lax.rem(q + t, n_layer)
        pl.semaphore_signal(barrier, inc=1, device_id=(other, to), device_id_type=MESH)

        @pl.when(t > 0)
        def _():
            pl.semaphore_signal(barrier, inc=1, device_id=(img, to), device_id_type=MESH)

    @pl.loop(1, 8)
    def _(j):
        w_load(j).start()

    loads[1].start()
    pl.semaphore_wait(barrier, 2 * n_layer - 1)

    def incoming(source, slot, first, count, n):
        return pltpu.make_async_remote_copy(
            src_ref=source.at[pl.ds(first, count)], dst_ref=x.at[pl.ds(slot * rows + first, count)],
            send_sem=in_send.at[n], recv_sem=in_recv.at[n],
            device_id=(other, q), device_id_type=MESH,
        )

    def start_in():
        return incoming(a_hbm, 4, 0, rows, 2)

    def cotan_in(h):
        return incoming(c_hbm, 7, pl.multiple_of(h * half, half), half, h)

    @pl.when(jnp.logical_not(holds))
    def _():
        start_in().start()

        @pl.loop(0, 2)
        def _(h):
            cotan_in(h).start()

    def self_copy(t):
        to = lax.rem(q + t, n_layer)
        return pltpu.make_async_remote_copy(
            src_ref=sums.at[0, pl.ds(pl.multiple_of(to * part, part), part)], dst_ref=self_in.at[q],
            send_sem=self_send.at[t], recv_sem=self_recv.at[q],
            device_id=(img, to), device_id_type=MESH,
        )

    def self_arrival(source):
        return pltpu.make_async_remote_copy(
            src_ref=sums.at[0, pl.ds(0, part)], dst_ref=self_in.at[source],
            send_sem=self_send.at[0], recv_sem=self_recv.at[source],
            device_id=(img, source), device_id_type=MESH,
        )

    def block_copy(b, source):
        return pltpu.make_async_remote_copy(
            src_ref=sums.at[1, pl.ds(pl.multiple_of(b * part, part), part)], dst_ref=cross_in.at[source],
            send_sem=block_send.at[b], recv_sem=block_recv.at[source],
            device_id=(other, b), device_id_type=MESH,
        )

    def piece_copy(b, t, source):
        to = lax.rem(q + t, n_layer)
        return pltpu.make_async_remote_copy(
            src_ref=piece_out.at[b, pl.ds(pl.multiple_of(to * part, part), part)],
            dst_ref=cross_in.at[source, :, pl.ds(pl.multiple_of(b * part, part), part)],
            send_sem=piece_send.at[b, t], recv_sem=piece_recv.at[source, b],
            device_id=(img, to), device_id_type=MESH,
        )

    loads[0].wait()

    @pl.loop(0, jnp.where(holds, 2, 1))
    def _(p):
        @pl.when(p == 1)
        def _():
            start_in().wait_recv()

        @pl.loop(0, 32)
        def _(j):
            k, n, h = lax.div(j, 16), lax.rem(lax.div(j, 2), 8), lax.rem(j, 2)
            at = pl.ds(pl.multiple_of(n * half, half), half)

            @pl.when(p + lax.rem(j, 4) == 0)
            def _():
                w_load(lax.div(j, 4)).wait()

            here = (4 * p + k) * rows + h * half
            v = dot(
                x[pl.ds(pl.multiple_of(here, half), half), :],
                x[pl.ds(pl.multiple_of(first_w + k * width, width), width), at],
                NN,
            )
            s = jax.nn.sigmoid(v)
            d[k, pl.ds(pl.multiple_of(h * half, half), half), at] = s * (1.0 + v * (1.0 - s))
            x[pl.ds(pl.multiple_of(here + rows, half), half), at] = (v * s).astype(BF16)

        @pl.when(p == 0)
        def _():
            loads[1].wait()

        @pl.loop(0, 3)
        def _(stage):
            opening = lax.div(2 - stage, 2)

            @pl.when(stage > 0)
            def _():
                h = stage - 1

                @pl.when(p == 1)
                def _():
                    cotan_in(h).wait_recv()

                @pl.loop(0, 2 * half // 16)
                def _(i):
                    m, n = lax.div(i, 2) * 16, lax.rem(i, 2) * (width // 2)
                    cols = pl.ds(pl.multiple_of(n, width // 2), width // 2)
                    at = pl.ds(pl.multiple_of((4 * p + 3) * rows + h * half + m, 16), 16)
                    z_at = pl.ds(pl.multiple_of(h * half + m, 16), 16)
                    x[at, cols] = (x[at, cols].astype(F32) * d[1, z_at, cols]).astype(BF16)

            @pl.loop(0, 12 - 4 * opening)
            def _(jj):
                j, e = lax.div(jj, 2), lax.rem(jj, 2)
                back = lax.div(7 - j, 4) * (1 - opening)
                k = opening * lax.div(j, 2) + (1 - opening) * (1 - back) * (7 - j)
                h = opening * lax.rem(j, 2) + (1 - opening) * (stage - 1)
                left = (4 * p + k + 3 * back) * rows + h * half
                right = back * (first_w + width + j * step) + (1 - back) * k * rows + e * half
                @pl.when(p + back + (h - e + 1) > 0)
                def _():
                    v = dot(
                        x[pl.ds(pl.multiple_of(left, half), half), :],
                        x[pl.ds(pl.multiple_of(right, half), half), :],
                        NT,
                    )
                    gram[back * 8 + (1 - back) * (2 * k + h), :, pl.ds(pl.multiple_of(e * half, half), half)] = v
                    cols = pl.ds(pl.multiple_of(back * j * step + e * half, half), half)
                    to = back * ((4 * p + 2) * rows + h * half) + (1 - back) * spare
                    slope = d[0, pl.ds(pl.multiple_of(h * half, half), half), cols]
                    x[pl.ds(pl.multiple_of(to, half), half), cols] = (v * slope).astype(BF16)

            @pl.when(stage > 0)
            def _():
                h = stage - 1

                @pl.loop(0, 2)
                def _(i):
                    b = 2 * h + i

                    @pl.loop(0, part // 16)
                    def _(m):
                        at = pl.ds(pl.multiple_of(i * part + m * 16, 16), 16)
                        sums[p, pl.ds(pl.multiple_of(b * part + m * 16, 16), 16), :] = (
                            gram[h, at, :] * scale
                        ) * (gram[4 + h, at, :] * scale) + (gram[2 + h, at, :] * scale) * (
                            gram[6 + h, at, :] * scale
                        )

                    @pl.when(p == 1)
                    def _():
                        block_copy(b, q).start()

                        @pl.loop(0, n_layer)
                        def _(m):
                            at = pl.ds(pl.multiple_of(m * part, part), part)
                            piece_out[b, at, :] = sums[1, pl.ds(pl.multiple_of(b * part, part), part), at].T

                        @pl.loop(1, n_layer)
                        def _(t):
                            piece_copy(b, t, q).start()

                        cross_in[q, :, pl.ds(pl.multiple_of(b * part, part), part)] = piece_out[
                            b, pl.ds(pl.multiple_of(q * part, part), part), :
                        ]

        @pl.when(p == 0)
        def _():
            @pl.loop(0, 4)
            def _(m):
                first, second = lax.div(m, 2) * part, half + lax.rem(m, 2) * part
                first = pl.ds(pl.multiple_of(first, part), part)
                second = pl.ds(pl.multiple_of(second, part), part)
                sums[0, first, second] = sums[0, second, first].T

            @pl.loop(1, n_layer)
            def _(t):
                self_copy(t).start()

    @pl.loop(1, n_layer)
    def _(t):
        self_arrival(lax.rem(q + t, n_layer)).wait_recv()

    @pl.loop(0, n_layer)
    def _(source):
        near = lax.rem(side + source, 2) == 0

        @pl.when(jnp.logical_and(near, q != source))
        def _():
            @pl.loop(0, n_layer)
            def _(b):
                piece_copy(b, 1, source).wait_recv()

        @pl.when(jnp.logical_not(near))
        def _():
            block_copy(0, source).wait_recv()

    @pl.loop(0, part // 16)
    def _(m):
        at = pl.ds(pl.multiple_of(m * 16, 16), 16)
        cross_out[at, :] = (cross_in[0, at, :] + cross_in[1, at, :]) + (cross_in[2, at, :] + cross_in[3, at, :])
        total = sums[0, pl.ds(pl.multiple_of(q * part + m * 16, 16), 16), :]
        for t in range(1, n_layer):
            total = total + self_in[lax.rem(q + t, n_layer), at, :]
        self_out[at, :] = total

    @pl.loop(1, n_layer)
    def _(t):
        self_copy(t).wait_send()

    @pl.when(holds)
    def _():
        @pl.loop(0, n_layer)
        def _(b):
            block_copy(b, q).wait_send()

            @pl.loop(1, n_layer)
            def _(t):
                piece_copy(b, t, q).wait_send()

    @pl.when(jnp.logical_not(holds))
    def _():
        start_in().wait_send()

        @pl.loop(0, 2)
        def _(h):
            cotan_in(h).wait_send()


def one_round(round_number, n_layer, a, c, w):
    rows, width = a.shape
    part = rows // n_layer
    dma = pltpu.SemaphoreType.DMA
    tile = jax.ShapeDtypeStruct((part, rows), F32)
    return pl.pallas_call(
        functools.partial(round_kernel, round_number, n_layer),
        out_shape=[tile, tile],
        in_specs=[pl.BlockSpec(memory_space=pl.ANY)] * 3,
        out_specs=[pl.BlockSpec(memory_space=pltpu.VMEM)] * 2,
        scratch_shapes=[
            pltpu.VMEM((8 * rows + 2 * width + rows // 2, width), BF16),
            pltpu.VMEM((2, rows, width), F32),
            pltpu.VMEM((9, rows // 2, rows), F32),
            pltpu.VMEM((2, rows, rows), F32),
            pltpu.VMEM((n_layer, rows, part), F32),
            pltpu.VMEM((n_layer, part, rows), F32),
            pltpu.VMEM((n_layer, part, rows), F32),
            dma((8,)), dma((2,)), dma((3,)), dma((3,)), dma((n_layer,)), dma((n_layer,)),
            dma((n_layer,)), dma((n_layer,)), dma((n_layer, n_layer)), dma((n_layer, n_layer)),
        ],
        compiler_params=pltpu.CompilerParams(
            collective_id=round_number, has_side_effects=True, vmem_limit_bytes=60 << 20
        ),
        cost_estimate=pl.CostEstimate(
            flops=8 * rows * width * width + 16 * rows * rows * width,
            bytes_accessed=2 * (w.size + 2 * a.size), transcendentals=4 * a.size,
        ),
        name=f"round_{round_number}",
    )(a, c, w)


def on_device(checkpoint, cotangent, weights, partner):
    round_number = jnp.bitwise_xor(partner[0], lax.axis_index("img"))
    n, n_layer = lax.axis_size("img"), lax.axis_size("layer")
    return tuple(
        lax.switch(
            round_number - 1,
            [functools.partial(one_round, r, n_layer) for r in range(1, n)],
            checkpoint[0], cotangent[0], weights,
        )
    )


def solution(mesh):
    return jax.shard_map(
        on_device,
        mesh=mesh,
        in_specs=(
            P("layer", "img", None),
            P("layer", "img", None),
            P("layer", None, None),
            P("img"),
        ),
        out_specs=(P(("img", "layer"), None), P(("img", "layer"), None)),
        check_vma=False,
    )
```
